32 devices in a mesh: box: 8 (over z, core), angle: 4 (over y, x).
Axes of the slice: x: 2, y: 2, z: 4, core: 2. Of those that a mesh axis runs over, the one named last changes fastest.
Arguments:
- coefficients: bfloat16 [2, 625, 49152], P(None, None, ('box', 'angle')), may hold values from -6 to 6
- plane_map: bfloat16 [2, 625, 2048], P(None, None, 'angle'), may hold values from -0.15625 to 0.15625
- leaf_parent: int32 [49152], P('box'), may hold values from -1 to 768, as said below
- leaf_octant: int32 [49152], P('box'), may hold values from 0 to 7, as said below
- box_parent: int32 [6144], P('box'), may hold values from -1 to 96, as said below
- box_octant: int32 [6144], P('box'), may hold values from 0 to 7, as said below
- interp_one: float32 [4, 4096], P(None, 'angle'), may hold values from 0.05 to 0.6
- phase_one: float32 [8, 4096], P(None, 'angle'), may hold values from -3.140625 to 3.140625
- interp_two: float32 [4, 8192], P(None, 'angle'), may hold values from 0.05 to 0.6
- phase_two: float32 [8, 8192], P(None, 'angle'), may hold values from -3.140625 to 3.140625
Outputs:
- signature_one: float32 [6144, 2, 4096], P('box', None, 'angle')
- signature_two: float32 [768, 2, 8192], P('box', None, 'angle')
The draws below stay inside these ranges and needn't reach their ends.
Inputs may be any that keep to these rules, and one draw needn't show every extreme that they name: `leaf_parent`: within each block of 6144 leaf slots: the slots with -1 come first, then live slots whose values never fall and name every slot from 0 to the block's live level-1 count minus 1, then slots with 768. Counting its children in both blocks, each level-1 box has 4 to 7 children. In every block but the last, the last live level-1 box has children in the next block, which hold that block's -1 slots; the first block has no -1 slot. A level-1 slot is named by some leaf exactly when its box_parent is not 96. `leaf_octant`: the children of one parent have distinct octants, rising along the slots; empty slots hold 0. `box_parent`: within each block of 768 level-1 slots: the slots with -1 come first, then live slots whose values never fall and name every slot from 0 to the block's level-2 count minus 1, then slots with 96. Counting its children in both blocks, each level-2 box has 4 to 7 children. In every block but the last, the last live level-2 box has children in the next block, which hold that block's -1 slots; the first block has no -1 slot. Some block uses all 96 level-2 slots. `box_octant`: the children of one parent have distinct octants, rising along the slots; empty slots hold 0.
All inputs are finite; a program needn't handle non-finite values.
Results may differ from the reference program's by a relative error of at most 0.0029.
Values may be sent and summed in bfloat16 or wider, within the bound.
A program may use at most 256 MiB of HBM per device.

```python
from functools import partial
import jax
import jax.numpy as jnp
from jax import lax

NC = 625
S0 = 2048
S1 = 4096
S2 = 8192
LEAF_DEV = 6144
LEAVES = 49152


def subset_table(key, group_sizes):
    scores = jax.random.randint(key, group_sizes.shape + (8,), 0, 1 << 20) * 8 + jnp.arange(8, dtype=jnp.int32)
    order = jnp.argsort(scores, axis=-1).astype(jnp.int32)
    masked = jnp.where(jnp.arange(8, dtype=jnp.int32) < group_sizes[..., None], order, 8)
    return jnp.sort(masked, axis=-1)


def place_slots(group_sizes, lead, total, prev_start, table, prev_row, slots, empty):
    ends = jnp.cumsum(group_sizes)
    starts = ends - group_sizes
    index = jnp.arange(slots, dtype=jnp.int32)
    offset = index - lead
    group = jnp.searchsorted(ends, offset, side='right').astype(jnp.int32)
    group = jnp.clip(group, 0, group_sizes.shape[0] - 1)
    position = jnp.clip(offset - starts[group], 0, 7)
    own_octant = table[group, position]
    lead_octant = prev_row[jnp.clip(prev_start + index, 0, 7)]
    parent = jnp.where(index < lead, -1, jnp.where(index < total, group, empty))
    octant = jnp.where(index < lead, lead_octant, jnp.where(index < total, own_octant, 0))
    return (parent.astype(jnp.int32), octant.astype(jnp.int32))


def build_level(key, groups, width, slots, empty, n_dev):
    key_sizes, key_tail, key_table = jax.random.split(key, 3)
    group_sizes = jax.random.randint(key_sizes, (n_dev, width), 4, 8)
    group_sizes = jnp.where(jnp.arange(width, dtype=jnp.int32)[None, :] < groups[:, None], group_sizes, 0)
    devices = jnp.arange(n_dev, dtype=jnp.int32)
    last_size = group_sizes[devices, groups - 1]
    tail = jax.random.randint(key_tail, (n_dev,), 1, last_size)
    tail = jnp.where(devices == n_dev - 1, 0, tail)
    lead = jnp.concatenate([jnp.zeros((1,), jnp.int32), tail[:-1]])
    total = lead + jnp.sum(group_sizes, axis=1) - tail
    table = subset_table(key_table, group_sizes)
    prev_row = jnp.roll(table[devices, groups - 1], 1, axis=0)
    prev_start = jnp.roll(last_size - tail, 1)
    placer = partial(place_slots, slots=slots, empty=empty)
    parent, octant = jax.vmap(placer)(group_sizes, lead, total, prev_start, table, prev_row)
    return (parent.reshape(-1), octant.reshape(-1), total)


def build_tree(key):
    n_dev = LEAVES // LEAF_DEV
    slots_one = LEAF_DEV // 8
    slots_two = LEAF_DEV // 64
    key_count, key_busy, key_upper, key_lower = jax.random.split(jax.random.fold_in(key, 4242), 4)
    groups = jax.random.randint(key_count, (n_dev,), 3 * slots_two // 4, slots_two + 1)
    busiest = jax.random.randint(key_busy, (), 0, n_dev)
    groups = jnp.where(jnp.arange(n_dev, dtype=jnp.int32) == busiest, slots_two, groups)
    box_parent, box_octant, owned = build_level(key_upper, groups, slots_two, slots_one, slots_two, n_dev)
    leaf_parent, leaf_octant, unused_total = build_level(key_lower, owned, slots_one, LEAF_DEV, slots_one, n_dev)
    return (leaf_parent, leaf_octant, box_parent, box_octant)


def draw_leaf_parent(key, part):
    return build_tree(key)[0]


def draw_leaf_octant(key, part):
    return build_tree(key)[1]


def draw_box_parent(key, part):
    return build_tree(key)[2]


def draw_box_octant(key, part):
    return build_tree(key)[3]


def level_of(own_key, shape, cuts, smallest, high):
    def one(axis_at, parts):
        heights = jax.random.uniform(jax.random.fold_in(jax.random.fold_in(own_key, 6), axis_at), (parts,), jnp.float32, smallest / len(cuts), high / len(cuts))
        return jnp.repeat(jnp.exp(heights), shape[axis_at] // parts).reshape((-1,) + (1,) * (len(shape) - axis_at - 1))

    level = one(*cuts[0])
    for cut in cuts[1:]:
        level = level * one(*cut)
    return level


def centred(rng, extent, deviation, reach, pieces=(), kind=jnp.bfloat16):
    loudness = level_of(rng, extent, pieces, -0.22, 0.18) if pieces else 1.0
    drawn = jax.random.normal(rng, extent, jnp.float32) * deviation * loudness
    return jnp.minimum(jnp.maximum(drawn, -reach), reach).astype(kind)


def setup_inputs(seed: int = 0) -> dict:
    seeds = jax.random.split(jax.random.key(seed), 11)
    return {
        "coefficients": centred(seeds[0], (2, NC, LEAVES), 1.0, 6.0, ((2, 32),)),
        "plane_map": centred(seeds[1], (2, NC, S0), (2 * NC) ** -0.5, 0.15625, ((2, 4),)),
        "leaf_parent": draw_leaf_parent(jax.random.fold_in(seeds[10], 71), 0),
        "leaf_octant": draw_leaf_octant(jax.random.fold_in(seeds[10], 71), 0),
        "box_parent": draw_box_parent(jax.random.fold_in(seeds[10], 71), 0),
        "box_octant": draw_box_octant(jax.random.fold_in(seeds[10], 71), 0),
        "interp_one": jnp.clip(0.05 + 0.55 * jax.random.uniform(seeds[6], (4, S1), jnp.float32) ** level_of(seeds[6], (4, S1), ((1, 4),), -0.2, 0.2), 0.05, 0.6),
        "phase_one": jnp.clip(jax.random.uniform(seeds[7], (8, S1), jnp.float32, -3.140625, 3.140625), -3.140625, 3.140625),
        "interp_two": jnp.clip(0.05 + 0.55 * jax.random.uniform(seeds[8], (4, S2), jnp.float32) ** level_of(seeds[8], (4, S2), ((1, 4),), -0.2, 0.2), 0.05, 0.6),
        "phase_two": jnp.clip(jax.random.uniform(seeds[9], (8, S2), jnp.float32, -3.140625, 3.140625), -3.140625, 3.140625),
    }


def real_form(block):
    real_part = block[0]
    imag_part = block[1]
    upper = jnp.concatenate([real_part, imag_part], axis=1)
    lower = jnp.concatenate([-imag_part, real_part], axis=1)
    return jnp.concatenate([upper, lower], axis=0)


def leaf_product(coef_block, weights):
    count = coef_block.shape[2]
    width = weights.shape[1] // 2
    flat = coef_block.reshape(coef_block.shape[0] * coef_block.shape[1], count)
    product = lax.dot_general(flat, weights, (((0,), (0,)), ((), ())), preferred_element_type=jnp.float32)
    return product.reshape(count, 2, width).astype(jnp.bfloat16)


def octant_rows(octant, table):
    selector = (octant[:, None] == jnp.arange(8, dtype=jnp.int32)[None, :]).astype(jnp.float32)
    return jnp.dot(selector, table, precision=lax.Precision.HIGHEST)


def upsample_shift(padded, weights, octant, cosine, sine):
    width = padded.shape[-1] - 4
    total = jnp.zeros(padded.shape[:-1] + (2 * width,), jnp.float32)
    for tap_index in range(4):
        window = padded[..., 1 + tap_index:1 + tap_index + width].astype(jnp.float32)
        total = total + weights[tap_index] * jnp.repeat(window, 2, axis=-1)
    cos_rows = octant_rows(octant, cosine)
    sin_rows = octant_rows(octant, sine)
    real_part = total[:, 0]
    imag_part = total[:, 1]
    return jnp.stack([real_part * cos_rows - imag_part * sin_rows,
                      real_part * sin_rows + imag_part * cos_rows], axis=1)


def wrap_pad(field):
    return jnp.concatenate([field[..., -2:], field, field[..., :2]], axis=-1)


def attach(owned, carried, last_slot):
    incoming = jnp.concatenate([carried[1:], jnp.zeros_like(carried[:1])], axis=0)
    slot_ids = jnp.arange(owned.shape[1], dtype=jnp.int32)
    selector = (slot_ids[None, :] == last_slot[:, None]).astype(jnp.float32)
    return owned + selector[:, :, None, None] * incoming[:, None]


def reference(coefficients, plane_map, leaf_parent, leaf_octant, box_parent, box_octant, interp_one, phase_one, interp_two, phase_two):
    n_dev = leaf_parent.shape[0] // LEAF_DEV
    slots_one = LEAF_DEV // 8
    slots_two = LEAF_DEV // 64
    weights = real_form(plane_map)
    cos_one = jnp.cos(phase_one)
    sin_one = jnp.sin(phase_one)
    cos_two = jnp.cos(phase_two)
    sin_two = jnp.sin(phase_two)
    parents_one = box_parent.reshape(n_dev, slots_one)
    octants_one = box_octant.reshape(n_dev, slots_one)

    def level_leaves(device):
        first = (device * LEAF_DEV).astype(jnp.int32)
        coef_block = lax.dynamic_slice_in_dim(coefficients, first, LEAF_DEV, 2)
        signature = leaf_product(coef_block, weights)
        parent = lax.dynamic_slice_in_dim(leaf_parent, first, LEAF_DEV, 0)
        octant = lax.dynamic_slice_in_dim(leaf_octant, first, LEAF_DEV, 0)
        contrib = upsample_shift(wrap_pad(signature), interp_one, octant, cos_one, sin_one)
        target = jnp.where(parent < 0, slots_one + 1, parent)
        sums = jax.ops.segment_sum(contrib, target, slots_one + 2)
        return sums[:slots_one], sums[slots_one + 1]

    owned, carried = lax.map(level_leaves, jnp.arange(n_dev, dtype=jnp.int32))
    live = jnp.sum((parents_one != slots_two).astype(jnp.int32), axis=1)
    signature_one = attach(owned, carried, live - 1)

    def level_boxes(inputs):
        field, parent, octant = inputs
        contrib = upsample_shift(wrap_pad(field), interp_two, octant, cos_two, sin_two)
        target = jnp.where(parent < 0, slots_two + 1, parent)
        sums = jax.ops.segment_sum(contrib, target, slots_two + 2)
        return sums[:slots_two], sums[slots_two + 1]

    owned_two, carried_two = lax.map(level_boxes, (signature_one, parents_one, octants_one))
    last_two = jnp.max(jnp.where(parents_one < slots_two, parents_one, -1), axis=1)
    signature_two = attach(owned_two, carried_two, last_two)
    return (signature_one.reshape(n_dev * slots_one, 2, signature_one.shape[-1]),
            signature_two.reshape(n_dev * slots_two, 2, signature_two.shape[-1]))
```

```python
import functools

import jax
import jax.numpy as jnp
from jax import lax
from jax.experimental import pallas as pl
from jax.experimental.pallas import tpu as pltpu
from jax.sharding import PartitionSpec as P

BF = jnp.bfloat16
F32 = jnp.float32
PAD = 128
CHUNK = 256


def passed_along(array, axis, by):
    peers = lax.axis_size(axis)
    pairs = [(i, i + by) for i in range(peers) if 0 <= i + by < peers]
    return lax.ppermute(array, axis, pairs)


def widened(cells, left, right, axis):
    count = lax.axis_size(axis)
    width = cells.shape[-1]
    head = cells[..., :right]
    tail = cells[..., width - left :]
    before = lax.ppermute(tail, axis, [(i, (i + 1) % count) for i in range(count)])
    after = lax.ppermute(head, axis, [((i + 1) % count, i) for i in range(count)])
    fill = jnp.zeros(cells.shape[:-1] + (PAD - left - right,), cells.dtype)
    return jnp.concatenate([before, cells, after, fill], axis=-1)


def split(array):
    high = array.astype(BF)
    return high, (array - high.astype(F32)).astype(BF)


def split_table(array):
    high = lax.reduce_precision(array, 8, 7)
    return high.astype(BF), (array - high).astype(BF)


def band(weights, shift):
    columns = weights.shape[1]
    rows = jnp.arange(CHUNK, dtype=jnp.int32)[:, None]
    first = (jnp.arange(columns, dtype=jnp.int32)[None, :] % CHUNK) // 2 + shift
    total = jnp.zeros((CHUNK, columns), F32)
    for tap in range(4):
        total = total + jnp.where(rows == first + tap, weights[tap][None, :], 0.0)
    return jnp.stack(split_table(total))


def phase_table(phase):
    both = jnp.concatenate([jnp.cos(phase), jnp.sin(phase)], axis=1)
    return jnp.concatenate(split_table(both), axis=0)


def dot(a, b):
    return jnp.dot(a, b, preferred_element_type=F32)


def dot_lead(a, b):
    return lax.dot_general(a, b, (((0,), (0,)), ((), ())), preferred_element_type=F32)


def octant_hot(octant):
    rows = lax.broadcasted_iota(jnp.int32, (16, octant.shape[1]), 0)
    return ((rows % 8) == octant).astype(F32).astype(BF)


def level_one_kernel(window, meta, coef, weights, bands, table, target, octant, sums, carry):
    tile = pl.program_id(0)
    wide = sums.shape[2]
    ext = weights.shape[2] // 2
    keep = window - 8

    @pl.when(tile == 0)
    def _():
        sums[...] = jnp.zeros_like(sums)

    @pl.when(tile < meta[0])
    def _():
        base = pl.multiple_of(meta[1 + tile], 8)
        leaf = dot_lead(coef[0, 0], weights[0]) + dot_lead(coef[0, 1], weights[1])
        leaf = leaf.astype(BF)
        count = leaf.shape[0]
        hot = octant_hot(octant[0])
        rows = lax.broadcasted_iota(jnp.int32, (window, count), 0)
        select = (rows == target[0] - base).astype(F32).astype(BF)
        for lo in range(0, wide, CHUNK):
            hi = min(lo + CHUNK, wide)
            start = lo // 2
            stop = min(start + CHUNK, ext)
            deep = stop - start
            wh = bands[0, :deep, lo:hi]
            wl = bands[1, :deep, lo:hi]
            xr = leaf[:, start:stop]
            xi = leaf[:, ext + start : ext + stop]
            ur = dot(xr, wh) + dot(xr, wl)
            ui = dot(xi, wh) + dot(xi, wl)
            cosine = dot_lead(hot, table[:, lo:hi])
            sine = dot_lead(hot, table[:, wide + lo : wide + hi])
            for part, value in ((0, ur * cosine - ui * sine), (1, ur * sine + ui * cosine)):
                res = dot(select, value.astype(BF))
                sums[part, pl.ds(base, keep), lo:hi] += res[:keep]

                @pl.when(tile == 0)
                def _():
                    carry[part, :, lo:hi] = res[keep:]


def level_one(gathered, weights, bands, table, leaf_parent, leaf_octant, slots_one):
    groups, _, order, per = gathered.shape
    leaves = groups * per
    tile = next(t for t in (256, 128) if per % t == 0)
    window = tile // 4 + 24
    tiles = leaves // tile
    each = per // tile
    wide = bands.shape[2]
    live = jnp.sum((leaf_parent != slots_one).astype(jnp.int32))
    live_tiles = (live + tile - 1) // tile
    first = leaf_parent.reshape(tiles, tile)[:, 0]
    base = jnp.clip(first, 0, slots_one - 1) // 8 * 8
    meta = jnp.concatenate([live_tiles[None], base]).astype(jnp.int32)
    target = jnp.where(
        leaf_parent == slots_one, -8, jnp.where(leaf_parent < 0, window - 1, leaf_parent)
    )

    def at(i, meta):
        return jnp.minimum(i, jnp.maximum(meta[0] - 1, 0))

    return pl.pallas_call(
        functools.partial(level_one_kernel, window),
        grid_spec=pltpu.PrefetchScalarGridSpec(
            num_scalar_prefetch=1,
            grid=(tiles,),
            in_specs=[
                pl.BlockSpec(
                    (1, 2, order, tile), lambda i, m: (at(i, m) // each, 0, 0, at(i, m) % each)
                ),
                pl.BlockSpec(weights.shape, lambda i, m: (0, 0, 0)),
                pl.BlockSpec(bands.shape, lambda i, m: (0, 0, 0)),
                pl.BlockSpec(table.shape, lambda i, m: (0, 0)),
                pl.BlockSpec((1, 1, tile), lambda i, m: (at(i, m), 0, 0)),
                pl.BlockSpec((1, 1, tile), lambda i, m: (at(i, m), 0, 0)),
            ],
            out_specs=[
                pl.BlockSpec((2, slots_one + window, wide), lambda i, m: (0, 0, 0)),
                pl.BlockSpec((2, 8, wide), lambda i, m: (0, 0, 0)),
            ],
        ),
        out_shape=[
            jax.ShapeDtypeStruct((2, slots_one + window, wide), F32),
            jax.ShapeDtypeStruct((2, 8, wide), F32),
        ],
        compiler_params=pltpu.CompilerParams(vmem_limit_bytes=56 * 2**20),
        cost_estimate=pl.CostEstimate(
            flops=2 * leaves * order * 8 * weights.shape[2],
            bytes_accessed=2 * gathered.size,
            transcendentals=0,
        ),
    )(
        meta,
        gathered,
        weights,
        bands,
        table,
        target.reshape(tiles, 1, tile),
        leaf_octant.reshape(tiles, 1, tile),
    )


def level_two_kernel(meta, sums, incoming, bands, table, target, octant, one, two):
    tile = pl.program_id(0)
    count = sums.shape[1]
    wide = bands.shape[2]
    near = one.shape[2]
    slots = lax.broadcasted_iota(jnp.int32, (count, 1), 0) + tile * count
    last = slots == meta[1]
    fields = []
    for part in range(2):
        field = sums[part] + jnp.where(last, incoming[part : part + 1], 0.0)
        fields.append(field)
        one[:, part, :] = field[:, 2 : 2 + near]

    @pl.when(tile == 0)
    def _():
        two[...] = jnp.zeros_like(two)

    @pl.when(tile < meta[0])
    def _():
        rows = two.shape[1]
        hot = octant_hot(octant[0])
        select = lax.broadcasted_iota(jnp.int32, (rows, count), 0) == target[0]
        select = select.astype(F32).astype(BF)
        halves = [split(field) for field in fields]
        for lo in range(0, wide, CHUNK):
            hi = min(lo + CHUNK, wide)
            start = lo // 2
            stop = start + CHUNK
            wh = bands[0, :, lo:hi]
            wl = bands[1, :, lo:hi]
            ups = []
            for xh, xl in halves:
                xh = xh[:, start:stop]
                ups.append(dot(xh, wh) + dot(xh, wl) + dot(xl[:, start:stop], wh))
            ur, ui = ups
            cosine = dot_lead(hot, table[:, lo:hi])
            sine = dot_lead(hot, table[:, wide + lo : wide + hi])
            for part, value in ((0, ur * cosine - ui * sine), (1, ur * sine + ui * cosine)):
                vh, vl = split(value)
                two[part, :, lo:hi] += dot(select, vh) + dot(select, vl)


def level_two(sums, incoming, live, bands, table, box_parent, box_octant, slots_two):
    slots_one = box_parent.shape[0]
    ext = sums.shape[2]
    tile = next(t for t in (128, 64, 32, 8) if slots_one % t == 0)
    tiles = slots_one // tile
    rows = (slots_two + 7) // 8 * 8 + 8
    wide = bands.shape[2]
    meta = jnp.stack([(live + tile - 1) // tile, live - 1]).astype(jnp.int32)
    target = jnp.where(
        box_parent == slots_two, -8, jnp.where(box_parent < 0, rows - 1, box_parent)
    )
    return pl.pallas_call(
        level_two_kernel,
        grid_spec=pltpu.PrefetchScalarGridSpec(
            num_scalar_prefetch=1,
            grid=(tiles,),
            in_specs=[
                pl.BlockSpec((2, tile, ext), lambda i, m: (0, i, 0)),
                pl.BlockSpec((2, ext), lambda i, m: (0, 0)),
                pl.BlockSpec(bands.shape, lambda i, m: (0, 0, 0)),
                pl.BlockSpec(table.shape, lambda i, m: (0, 0)),
                pl.BlockSpec((1, 1, tile), lambda i, m: (i, 0, 0)),
                pl.BlockSpec((1, 1, tile), lambda i, m: (i, 0, 0)),
            ],
            out_specs=[
                pl.BlockSpec((tile, 2, ext - PAD), lambda i, m: (i, 0, 0)),
                pl.BlockSpec((2, rows, wide), lambda i, m: (0, 0, 0)),
            ],
        ),
        out_shape=[
            jax.ShapeDtypeStruct((slots_one, 2, ext - PAD), F32),
            jax.ShapeDtypeStruct((2, rows, wide), F32),
        ],
        compiler_params=pltpu.CompilerParams(vmem_limit_bytes=56 * 2**20),
    )(
        meta,
        sums,
        incoming,
        bands,
        table,
        target.reshape(tiles, 1, tile),
        box_octant.reshape(tiles, 1, tile),
    )


def body(
    coefficients,
    plane_map,
    leaf_parent,
    leaf_octant,
    box_parent,
    box_octant,
    interp_one,
    phase_one,
    interp_two,
    phase_two,
):
    slots_one = box_parent.shape[0]
    slots_two = slots_one // 8
    gathered = lax.all_gather(coefficients, "angle", axis=0)
    plane = widened(plane_map, 2, 3, "angle")
    weights = jnp.stack(
        [
            jnp.concatenate([plane[0], plane[1]], axis=1),
            jnp.concatenate([-plane[1], plane[0]], axis=1),
        ]
    )
    near = widened(jnp.concatenate([interp_one, phase_one], axis=0), 2, 2, "angle")
    sums, carry = level_one(
        gathered,
        weights,
        band(near[:4], 0),
        phase_table(near[4:]),
        leaf_parent,
        leaf_octant,
        slots_one,
    )
    incoming = passed_along(carry[:, 7], "box", -1)
    live = jnp.sum((box_parent != slots_two).astype(jnp.int32))
    signature_one, sums_two = level_two(
        sums,
        incoming,
        live,
        band(interp_two, 1),
        phase_table(phase_two),
        box_parent,
        box_octant,
        slots_two,
    )
    incoming_two = passed_along(sums_two[:, -1], "box", -1)
    last_two = jnp.max(jnp.where(box_parent < slots_two, box_parent, -1))
    hit = jnp.arange(slots_two, dtype=jnp.int32)[:, None, None] == last_two
    signature_two = jnp.swapaxes(sums_two[:, :slots_two], 0, 1) + jnp.where(
        hit, incoming_two[None], 0.0
    )
    return (signature_one, signature_two)


def solution(mesh):
    in_specs = (
        P(None, None, ("box", "angle")),
        P(None, None, "angle"),
        P("box"),
        P("box"),
        P("box"),
        P("box"),
        P(None, "angle"),
        P(None, "angle"),
        P(None, "angle"),
        P(None, "angle"),
    )
    out_specs = (P("box", None, "angle"), P("box", None, "angle"))
    return jax.shard_map(body, mesh=mesh, in_specs=in_specs, out_specs=out_specs, check_vma=False)
```

```python
import functools

import jax
import jax.numpy as jnp
from jax import lax
from jax.experimental import pallas as pl
from jax.experimental.pallas import tpu as pltpu
from jax.sharding import PartitionSpec as P

BF = jnp.bfloat16
F32 = jnp.float32
PAD = 128
CHUNK = 256


def passed_along(array, axis, by):
    peers = lax.axis_size(axis)
    pairs = [(i, i + by) for i in range(peers) if 0 <= i + by < peers]
    return lax.ppermute(array, axis, pairs)


def widened(cells, left, right, axis):
    count = lax.axis_size(axis)
    width = cells.shape[-1]
    head = cells[..., :right]
    tail = cells[..., width - left :]
    before = lax.ppermute(tail, axis, [(i, (i + 1) % count) for i in range(count)])
    after = lax.ppermute(head, axis, [((i + 1) % count, i) for i in range(count)])
    fill = jnp.zeros(cells.shape[:-1] + (PAD - left - right,), cells.dtype)
    return jnp.concatenate([before, cells, after, fill], axis=-1)


def split(array):
    high = array.astype(BF)
    return high, (array - high.astype(F32)).astype(BF)


def split_table(array):
    high = lax.reduce_precision(array, 8, 7)
    return high.astype(BF), (array - high).astype(BF)


def band(weights, shift):
    columns = weights.shape[1]
    rows = jnp.arange(CHUNK, dtype=jnp.int32)[:, None]
    first = (jnp.arange(columns, dtype=jnp.int32)[None, :] % CHUNK) // 2 + shift
    total = jnp.zeros((CHUNK, columns), F32)
    for tap in range(4):
        total = total + jnp.where(rows == first + tap, weights[tap][None, :], 0.0)
    return jnp.stack(split_table(total))


def phase_table(phase):
    both = jnp.concatenate([jnp.cos(phase), jnp.sin(phase)], axis=1)
    return jnp.concatenate(split_table(both), axis=0)


def dot(a, b):
    return jnp.dot(a, b, preferred_element_type=F32)


def dot_lead(a, b):
    return lax.dot_general(a, b, (((0,), (0,)), ((), ())), preferred_element_type=F32)


def octant_hot(octant):
    rows = lax.broadcasted_iota(jnp.int32, (16, octant.shape[1]), 0)
    return ((rows % 8) == octant).astype(F32).astype(BF)


def leaf_tile(window, tile, meta, coef, weights, bands, table, target, octant, sums, carry):
    wide = sums.shape[2]
    ext = weights.shape[2] // 2
    keep = window - 8

    @pl.when(tile < meta[0])
    def _():
        base = pl.multiple_of(meta[1 + tile], 8)
        leaf = dot_lead(coef[0], weights[0]) + dot_lead(coef[1], weights[1])
        leaf = leaf.astype(BF)
        count = leaf.shape[0]
        hot = octant_hot(octant[tile])
        rows = lax.broadcasted_iota(jnp.int32, (window, count), 0)
        select = (rows == target[tile] - base).astype(F32).astype(BF)
        for lo in range(0, wide, CHUNK):
            hi = min(lo + CHUNK, wide)
            start = lo // 2
            stop = min(start + CHUNK, ext)
            deep = stop - start
            wh = bands[0, :deep, lo:hi]
            wl = bands[1, :deep, lo:hi]
            xr = leaf[:, start:stop]
            xi = leaf[:, ext + start : ext + stop]
            ur = dot(xr, wh) + dot(xr, wl)
            ui = dot(xi, wh) + dot(xi, wl)
            cosine = dot_lead(hot, table[:, lo:hi])
            sine = dot_lead(hot, table[:, wide + lo : wide + hi])
            for part, value in ((0, ur * cosine - ui * sine), (1, ur * sine + ui * cosine)):
                res = dot(select, value.astype(BF))
                sums[part, pl.ds(base, keep), lo:hi] += res[:keep]
                if carry is not None:

                    @pl.when(tile == 0)
                    def _():
                        carry[part, :, lo:hi] = res[keep:]


def whole_kernel(window, meta, coef, weights, bands, table, target, octant, sums, carry):
    tile = pl.program_id(0)

    @pl.when(tile == 0)
    def _():
        sums[...] = jnp.zeros_like(sums)

    leaf_tile(
        window, tile, meta, coef.at[0], weights, bands, table, target, octant, sums, carry
    )


def pair_kernel(window, tiles, meta, left, right, weights, bands, table, target, octant, *refs):
    if len(refs) == 2 and refs[1].shape[1] == 8:
        sums, carry = refs
        sums[...] = jnp.zeros_like(sums)
    else:
        before, sums = refs
        carry = None
        sums[...] = before[...]
    for place, coef in enumerate((left, right)):
        tile = meta[1 + tiles + place]
        leaf_tile(window, tile, meta, coef, weights, bands, table, target, octant, sums, carry)


def tile_of(per):
    return next(t for t in (256, 128) if per % t == 0)


def window_of(tile):
    return tile // 4 + 24


def leaf_plan(leaf_parent, leaf_octant, slots_one, live, tile):
    tiles = leaf_parent.shape[0] // tile
    first = leaf_parent.reshape(tiles, tile)[:, 0]
    base = jnp.clip(first, 0, slots_one - 1) // 8 * 8
    meta = jnp.concatenate([((live + tile - 1) // tile)[None], base]).astype(jnp.int32)
    target = jnp.where(
        leaf_parent == slots_one,
        -8,
        jnp.where(leaf_parent < 0, window_of(tile) - 1, leaf_parent),
    )
    return meta, target.reshape(tiles, 1, tile), leaf_octant.reshape(tiles, 1, tile)


def full_spec(array):
    zeros = (0,) * array.ndim
    return pl.BlockSpec(array.shape, lambda i, m: zeros)


def level_one_whole(gathered, consts, meta, slots_one):
    groups, _, order, per = gathered.shape
    weights, bands, table, target, octant = consts
    tile = target.shape[2]
    window = window_of(tile)
    each = per // tile
    wide = bands.shape[2]

    def at(i, meta):
        return jnp.minimum(i, jnp.maximum(meta[0] - 1, 0))

    outs = [
        jax.ShapeDtypeStruct((2, slots_one + window, wide), F32),
        jax.ShapeDtypeStruct((2, 8, wide), F32),
    ]
    return pl.pallas_call(
        functools.partial(whole_kernel, window),
        grid_spec=pltpu.PrefetchScalarGridSpec(
            num_scalar_prefetch=1,
            grid=(groups * each,),
            in_specs=[
                pl.BlockSpec(
                    (1, 2, order, tile), lambda i, m: (at(i, m) // each, 0, 0, at(i, m) % each)
                )
            ]
            + [full_spec(c) for c in consts],
            out_specs=[full_spec(o) for o in outs],
        ),
        out_shape=outs,
        compiler_params=pltpu.CompilerParams(vmem_limit_bytes=56 * 2**20),
        cost_estimate=pl.CostEstimate(
            flops=16 * groups * per * order * weights.shape[2],
            bytes_accessed=2 * gathered.size,
            transcendentals=0,
        ),
    )(meta, gathered, *consts)


def level_one_pair(left, right, before, consts, meta, tiles, slots_one):
    weights, bands, table, target, octant = consts
    tile = target.shape[2]
    window = window_of(tile)
    wide = bands.shape[2]
    outs = [jax.ShapeDtypeStruct((2, slots_one + window, wide), F32)]
    operands = [left, right, *consts]
    if before is None:
        outs.append(jax.ShapeDtypeStruct((2, 8, wide), F32))
    else:
        operands.append(before)
    return pl.pallas_call(
        functools.partial(pair_kernel, window, tiles),
        grid_spec=pltpu.PrefetchScalarGridSpec(
            num_scalar_prefetch=1,
            grid=(1,),
            in_specs=[full_spec(c) for c in operands],
            out_specs=[full_spec(o) for o in outs],
        ),
        out_shape=outs,
        compiler_params=pltpu.CompilerParams(vmem_limit_bytes=56 * 2**20),
        cost_estimate=pl.CostEstimate(
            flops=16 * 2 * tile * left.shape[1] * weights.shape[2],
            bytes_accessed=8 * outs[0].size,
            transcendentals=0,
        ),
    )(meta, *operands)


def level_two_kernel(meta, sums, incoming, bands, table, target, octant, one, two):
    tile = pl.program_id(0)
    count = sums.shape[1]
    wide = bands.shape[2]
    near = one.shape[2]
    slots = lax.broadcasted_iota(jnp.int32, (count, 1), 0) + tile * count
    last = slots == meta[1]
    fields = []
    for part in range(2):
        field = sums[part] + jnp.where(last, incoming[part : part + 1], 0.0)
        fields.append(field)
        one[:, part, :] = field[:, 2 : 2 + near]

    @pl.when(tile == 0)
    def _():
        two[...] = jnp.zeros_like(two)

    @pl.when(tile < meta[0])
    def _():
        rows = two.shape[1]
        hot = octant_hot(octant[0])
        select = lax.broadcasted_iota(jnp.int32, (rows, count), 0) == target[0]
        select = select.astype(F32).astype(BF)
        halves = [split(field) for field in fields]
        for lo in range(0, wide, CHUNK):
            hi = min(lo + CHUNK, wide)
            start = lo // 2
            stop = start + CHUNK
            wh = bands[0, :, lo:hi]
            wl = bands[1, :, lo:hi]
            ups = []
            for xh, xl in halves:
                xh = xh[:, start:stop]
                ups.append(dot(xh, wh) + dot(xh, wl) + dot(xl[:, start:stop], wh))
            ur, ui = ups
            cosine = dot_lead(hot, table[:, lo:hi])
            sine = dot_lead(hot, table[:, wide + lo : wide + hi])
            for part, value in ((0, ur * cosine - ui * sine), (1, ur * sine + ui * cosine)):
                vh, vl = split(value)
                two[part, :, lo:hi] += dot(select, vh) + dot(select, vl)


def level_two(sums, incoming, live, bands, table, box_parent, box_octant, slots_two):
    slots_one = box_parent.shape[0]
    ext = sums.shape[2]
    tile = next(t for t in (128, 64, 32, 8) if slots_one % t == 0)
    tiles = slots_one // tile
    rows = (slots_two + 7) // 8 * 8 + 8
    wide = bands.shape[2]
    meta = jnp.stack([(live + tile - 1) // tile, live - 1]).astype(jnp.int32)
    target = jnp.where(
        box_parent == slots_two, -8, jnp.where(box_parent < 0, rows - 1, box_parent)
    )
    return pl.pallas_call(
        level_two_kernel,
        grid_spec=pltpu.PrefetchScalarGridSpec(
            num_scalar_prefetch=1,
            grid=(tiles,),
            in_specs=[
                pl.BlockSpec((2, tile, ext), lambda i, m: (0, i, 0)),
                pl.BlockSpec((2, ext), lambda i, m: (0, 0)),
                pl.BlockSpec(bands.shape, lambda i, m: (0, 0, 0)),
                pl.BlockSpec(table.shape, lambda i, m: (0, 0)),
                pl.BlockSpec((1, 1, tile), lambda i, m: (i, 0, 0)),
                pl.BlockSpec((1, 1, tile), lambda i, m: (i, 0, 0)),
            ],
            out_specs=[
                pl.BlockSpec((tile, 2, ext - PAD), lambda i, m: (i, 0, 0)),
                pl.BlockSpec((2, rows, wide), lambda i, m: (0, 0, 0)),
            ],
        ),
        out_shape=[
            jax.ShapeDtypeStruct((slots_one, 2, ext - PAD), F32),
            jax.ShapeDtypeStruct((2, rows, wide), F32),
        ],
        compiler_params=pltpu.CompilerParams(vmem_limit_bytes=56 * 2**20),
    )(
        meta,
        sums,
        incoming,
        bands,
        table,
        target.reshape(tiles, 1, tile),
        box_octant.reshape(tiles, 1, tile),
    )


def body(
    coefficients,
    plane_map,
    leaf_parent,
    leaf_octant,
    box_parent,
    box_octant,
    interp_one,
    phase_one,
    interp_two,
    phase_two,
):
    slots_one = box_parent.shape[0]
    slots_two = slots_one // 8
    count = lax.axis_size("angle")
    me = lax.axis_index("angle")
    per = coefficients.shape[2]
    tile = tile_of(per)
    steps = per // tile
    tiles = leaf_parent.shape[0] // tile
    live_leaves = jnp.sum((leaf_parent != slots_one).astype(jnp.int32))

    def near_share(step):
        own = coefficients[:, :, step * tile : (step + 1) * tile]
        got = lax.ppermute(own, "angle", [(0, 2), (1, 3)])
        return jnp.where(me < 2, own, got)

    def swapped(array):
        return lax.ppermute(array, "angle", [(0, 1), (1, 0), (2, 3), (3, 2)])

    quick = count == 4
    ahead = min(2, steps)
    if quick:
        most = lax.pmax(live_leaves, "box")
        early = [near_share(step) for step in range(ahead)]
        early_swap = swapped(early[0])
    plane = widened(plane_map, 2, 3, "angle")
    weights = jnp.stack(
        [
            jnp.concatenate([plane[0], plane[1]], axis=1),
            jnp.concatenate([-plane[1], plane[0]], axis=1),
        ]
    )
    near = widened(jnp.concatenate([interp_one, phase_one], axis=0), 2, 2, "angle")
    meta, target, octant = leaf_plan(leaf_parent, leaf_octant, slots_one, live_leaves, tile)
    consts = (weights, band(near[:4], 0), phase_table(near[4:]), target, octant)

    def all_shares():
        gathered = lax.all_gather(coefficients, "angle", axis=0)
        return tuple(level_one_whole(gathered, consts, meta, slots_one))

    def two_shares():
        mine = lax.rem(me, 2)
        lefts = early + [near_share(step) for step in range(ahead, steps)]
        sums = None
        for step, left in enumerate(lefts):
            right = early_swap if step == 0 else swapped(left)
            places = jnp.stack([mine * steps + step, (1 - mine) * steps + step])
            order = jnp.concatenate([meta, places.astype(jnp.int32)])
            out = level_one_pair(left, right, sums, consts, order, tiles, slots_one)
            sums = out[0]
            if step == 0:
                carry = out[1]
        return sums, carry

    if quick:
        sums, carry = lax.cond(most <= 2 * per, two_shares, all_shares)
    else:
        sums, carry = all_shares()
    incoming = passed_along(carry[:, 7], "box", -1)
    live = jnp.sum((box_parent != slots_two).astype(jnp.int32))
    signature_one, sums_two = level_two(
        sums,
        incoming,
        live,
        band(interp_two, 1),
        phase_table(phase_two),
        box_parent,
        box_octant,
        slots_two,
    )
    incoming_two = passed_along(sums_two[:, -1], "box", -1)
    last_two = jnp.max(jnp.where(box_parent < slots_two, box_parent, -1))
    hit = jnp.arange(slots_two, dtype=jnp.int32)[:, None, None] == last_two
    signature_two = jnp.swapaxes(sums_two[:, :slots_two], 0, 1) + jnp.where(
        hit, incoming_two[None], 0.0
    )
    return (signature_one, signature_two)


def solution(mesh):
    in_specs = (
        P(None, None, ("box", "angle")),
        P(None, None, "angle"),
        P("box"),
        P("box"),
        P("box"),
        P("box"),
        P(None, "angle"),
        P(None, "angle"),
        P(None, "angle"),
        P(None, "angle"),
    )
    out_specs = (P("box", None, "angle"), P("box", None, "angle"))
    return jax.shard_map(body, mesh=mesh, in_specs=in_specs, out_specs=out_specs, check_vma=False)
```

```python
import functools

import jax
import jax.numpy as jnp
from jax import lax
from jax.experimental import pallas as pl
from jax.experimental.pallas import tpu as pltpu
from jax.sharding import PartitionSpec as P

BF = jnp.bfloat16
F32 = jnp.float32
PAD = 128
CHUNK = 256


def passed_along(array, axis, by):
    peers = lax.axis_size(axis)
    pairs = [(i, i + by) for i in range(peers) if 0 <= i + by < peers]
    return lax.ppermute(array, axis, pairs)


def widened(cells, left, right, axis):
    count = lax.axis_size(axis)
    width = cells.shape[-1]
    head = cells[..., :right]
    tail = cells[..., width - left :]
    before = lax.ppermute(tail, axis, [(i, (i + 1) % count) for i in range(count)])
    after = lax.ppermute(head, axis, [((i + 1) % count, i) for i in range(count)])
    fill = jnp.zeros(cells.shape[:-1] + (PAD - left - right,), cells.dtype)
    return jnp.concatenate([before, cells, after, fill], axis=-1)


def split(array):
    high = array.astype(BF)
    return high, (array - high.astype(F32)).astype(BF)


def split_table(array):
    high = lax.reduce_precision(array, 8, 7)
    return high.astype(BF), (array - high).astype(BF)


def band(weights, shift):
    columns = weights.shape[1]
    rows = jnp.arange(CHUNK, dtype=jnp.int32)[:, None]
    first = (jnp.arange(columns, dtype=jnp.int32)[None, :] % CHUNK) // 2 + shift
    total = jnp.zeros((CHUNK, columns), F32)
    for tap in range(4):
        total = total + jnp.where(rows == first + tap, weights[tap][None, :], 0.0)
    return jnp.stack(split_table(total))


def phase_table(phase):
    both = jnp.concatenate([jnp.cos(phase), jnp.sin(phase)], axis=1)
    return jnp.concatenate(split_table(both), axis=0)


def dot(a, b):
    return jnp.dot(a, b, preferred_element_type=F32)


def dot_lead(a, b):
    return lax.dot_general(a, b, (((0,), (0,)), ((), ())), preferred_element_type=F32)


def octant_hot(octant):
    rows = lax.broadcasted_iota(jnp.int32, (16, octant.shape[1]), 0)
    return ((rows % 8) == octant).astype(F32).astype(BF)


def leaf_tile(window, tile, meta, coef, weights, bands, table, target, octant, sums, carry):
    wide = sums.shape[2]
    ext = weights.shape[1] // 2
    keep = window - 8

    @pl.when(tile < meta[0])
    def _():
        base = pl.multiple_of(meta[1 + tile], 8)
        leaf = dot_lead(coef[...], weights[...]).astype(BF)
        count = leaf.shape[0]
        hot = octant_hot(octant[tile])
        rows = lax.broadcasted_iota(jnp.int32, (window, count), 0)
        select = (rows == target[tile] - base).astype(F32).astype(BF)
        for lo in range(0, wide, CHUNK):
            hi = min(lo + CHUNK, wide)
            start = lo // 2
            stop = min(start + CHUNK, ext)
            deep = stop - start
            wh = bands[0, :deep, lo:hi]
            wl = bands[1, :deep, lo:hi]
            xr = leaf[:, start:stop]
            xi = leaf[:, ext + start : ext + stop]
            ur = dot(xr, wh) + dot(xr, wl)
            ui = dot(xi, wh) + dot(xi, wl)
            cosine = dot_lead(hot, table[:, lo:hi])
            sine = dot_lead(hot, table[:, wide + lo : wide + hi])
            for part, value in ((0, ur * cosine - ui * sine), (1, ur * sine + ui * cosine)):
                res = dot(select, value.astype(BF))
                sums[part, pl.ds(base, keep), lo:hi] += res[:keep]
                if carry is not None:

                    @pl.when(tile == 0)
                    def _():
                        carry[part, :, lo:hi] = res[keep:]


def whole_kernel(window, meta, coef, weights, bands, table, target, octant, sums, carry):
    tile = pl.program_id(0)

    @pl.when(tile == 0)
    def _():
        sums[...] = jnp.zeros_like(sums)

    leaf_tile(
        window, tile, meta, coef.at[0], weights, bands, table, target, octant, sums, carry
    )


def pair_kernel(window, tiles, meta, left, right, weights, bands, table, target, octant, *refs):
    if len(refs) == 2 and refs[1].shape[1] == 8:
        sums, carry = refs
        sums[...] = jnp.zeros_like(sums)
    else:
        before, sums = refs
        carry = None
        sums[...] = before[...]
    for place, coef in enumerate((left, right)):
        tile = meta[1 + tiles + place]
        leaf_tile(window, tile, meta, coef, weights, bands, table, target, octant, sums, carry)


def tile_of(per):
    return next(t for t in (256, 128) if per % t == 0)


def window_of(tile):
    return tile // 4 + 24


def leaf_plan(leaf_parent, leaf_octant, slots_one, live, tile):
    tiles = leaf_parent.shape[0] // tile
    first = leaf_parent.reshape(tiles, tile)[:, 0]
    base = jnp.clip(first, 0, slots_one - 1) // 8 * 8
    meta = jnp.concatenate([((live + tile - 1) // tile)[None], base]).astype(jnp.int32)
    target = jnp.where(
        leaf_parent == slots_one,
        -8,
        jnp.where(leaf_parent < 0, window_of(tile) - 1, leaf_parent),
    )
    return meta, target.reshape(tiles, 1, tile), leaf_octant.reshape(tiles, 1, tile)


def full_spec(array):
    zeros = (0,) * array.ndim
    return pl.BlockSpec(array.shape, lambda i, m: zeros)


def level_one_whole(gathered, consts, meta, slots_one):
    groups, order, per = gathered.shape
    weights, bands, table, target, octant = consts
    tile = target.shape[2]
    window = window_of(tile)
    each = per // tile
    wide = bands.shape[2]

    def at(i, meta):
        return jnp.minimum(i, jnp.maximum(meta[0] - 1, 0))

    outs = [
        jax.ShapeDtypeStruct((2, slots_one + window, wide), F32),
        jax.ShapeDtypeStruct((2, 8, wide), F32),
    ]
    return pl.pallas_call(
        functools.partial(whole_kernel, window),
        grid_spec=pltpu.PrefetchScalarGridSpec(
            num_scalar_prefetch=1,
            grid=(groups * each,),
            in_specs=[
                pl.BlockSpec(
                    (1, order, tile), lambda i, m: (at(i, m) // each, 0, at(i, m) % each)
                )
            ]
            + [full_spec(c) for c in consts],
            out_specs=[full_spec(o) for o in outs],
        ),
        out_shape=outs,
        compiler_params=pltpu.CompilerParams(vmem_limit_bytes=56 * 2**20),
        cost_estimate=pl.CostEstimate(
            flops=8 * groups * per * order * weights.shape[1],
            bytes_accessed=2 * gathered.size,
            transcendentals=0,
        ),
    )(meta, gathered, *consts)


def level_one_pair(left, right, before, consts, meta, tiles, slots_one):
    weights, bands, table, target, octant = consts
    tile = target.shape[2]
    window = window_of(tile)
    wide = bands.shape[2]
    outs = [jax.ShapeDtypeStruct((2, slots_one + window, wide), F32)]
    operands = [left, right, *consts]
    if before is None:
        outs.append(jax.ShapeDtypeStruct((2, 8, wide), F32))
    else:
        operands.append(before)
    return pl.pallas_call(
        functools.partial(pair_kernel, window, tiles),
        grid_spec=pltpu.PrefetchScalarGridSpec(
            num_scalar_prefetch=1,
            grid=(1,),
            in_specs=[full_spec(c) for c in operands],
            out_specs=[full_spec(o) for o in outs],
        ),
        out_shape=outs,
        compiler_params=pltpu.CompilerParams(vmem_limit_bytes=56 * 2**20),
        cost_estimate=pl.CostEstimate(
            flops=4 * tile * left.shape[0] * weights.shape[1],
            bytes_accessed=8 * outs[0].size,
            transcendentals=0,
        ),
    )(meta, *operands)


def level_two_kernel(meta, sums, incoming, bands, table, target, octant, one, two):
    tile = pl.program_id(0)
    count = sums.shape[1]
    wide = bands.shape[2]
    near = one.shape[2]
    slots = lax.broadcasted_iota(jnp.int32, (count, 1), 0) + tile * count
    last = slots == meta[1]
    fields = []
    for part in range(2):
        field = sums[part] + jnp.where(last, incoming[part : part + 1], 0.0)
        fields.append(field)
        one[:, part, :] = field[:, 2 : 2 + near]

    @pl.when(tile == 0)
    def _():
        two[...] = jnp.zeros_like(two)

    @pl.when(tile < meta[0])
    def _():
        rows = two.shape[1]
        hot = octant_hot(octant[0])
        select = lax.broadcasted_iota(jnp.int32, (rows, count), 0) == target[0]
        select = select.astype(F32).astype(BF)
        halves = [split(field) for field in fields]
        for lo in range(0, wide, CHUNK):
            hi = min(lo + CHUNK, wide)
            start = lo // 2
            stop = start + CHUNK
            wh = bands[0, :, lo:hi]
            wl = bands[1, :, lo:hi]
            ups = []
            for xh, xl in halves:
                xh = xh[:, start:stop]
                ups.append(dot(xh, wh) + dot(xh, wl) + dot(xl[:, start:stop], wh))
            ur, ui = ups
            cosine = dot_lead(hot, table[:, lo:hi])
            sine = dot_lead(hot, table[:, wide + lo : wide + hi])
            for part, value in ((0, ur * cosine - ui * sine), (1, ur * sine + ui * cosine)):
                vh, vl = split(value)
                two[part, :, lo:hi] += dot(select, vh) + dot(select, vl)


def level_two(sums, incoming, live, bands, table, box_parent, box_octant, slots_two):
    slots_one = box_parent.shape[0]
    ext = sums.shape[2]
    tile = next(t for t in (128, 64, 32, 8) if slots_one % t == 0)
    tiles = slots_one // tile
    rows = (slots_two + 7) // 8 * 8 + 8
    wide = bands.shape[2]
    meta = jnp.stack([(live + tile - 1) // tile, live - 1]).astype(jnp.int32)
    target = jnp.where(
        box_parent == slots_two, -8, jnp.where(box_parent < 0, rows - 1, box_parent)
    )
    return pl.pallas_call(
        level_two_kernel,
        grid_spec=pltpu.PrefetchScalarGridSpec(
            num_scalar_prefetch=1,
            grid=(tiles,),
            in_specs=[
                pl.BlockSpec((2, tile, ext), lambda i, m: (0, i, 0)),
                pl.BlockSpec((2, ext), lambda i, m: (0, 0)),
                pl.BlockSpec(bands.shape, lambda i, m: (0, 0, 0)),
                pl.BlockSpec(table.shape, lambda i, m: (0, 0)),
                pl.BlockSpec((1, 1, tile), lambda i, m: (i, 0, 0)),
                pl.BlockSpec((1, 1, tile), lambda i, m: (i, 0, 0)),
            ],
            out_specs=[
                pl.BlockSpec((tile, 2, ext - PAD), lambda i, m: (i, 0, 0)),
                pl.BlockSpec((2, rows, wide), lambda i, m: (0, 0, 0)),
            ],
        ),
        out_shape=[
            jax.ShapeDtypeStruct((slots_one, 2, ext - PAD), F32),
            jax.ShapeDtypeStruct((2, rows, wide), F32),
        ],
        compiler_params=pltpu.CompilerParams(vmem_limit_bytes=56 * 2**20),
    )(
        meta,
        sums,
        incoming,
        bands,
        table,
        target.reshape(tiles, 1, tile),
        box_octant.reshape(tiles, 1, tile),
    )


def body(
    coefficients,
    plane_map,
    leaf_parent,
    leaf_octant,
    box_parent,
    box_octant,
    interp_one,
    phase_one,
    interp_two,
    phase_two,
):
    slots_one = box_parent.shape[0]
    slots_two = slots_one // 8
    count = lax.axis_size("angle")
    me = lax.axis_index("angle")
    per = coefficients.shape[2]
    tile = tile_of(per)
    steps = per // tile
    tiles = leaf_parent.shape[0] // tile
    live_leaves = jnp.sum((leaf_parent != slots_one).astype(jnp.int32))

    order = coefficients.shape[1]
    rows = (order + 7) // 8 * 8

    def flat():
        padded = jnp.pad(coefficients, ((0, 0), (0, rows - order), (0, 0)))
        return padded.reshape(2 * rows, per)

    def prepared():
        plane = jnp.pad(plane_map, ((0, 0), (0, rows - order), (0, 0)))
        plane = widened(plane, 2, 3, "angle")
        weights = jnp.concatenate(
            [
                jnp.concatenate([plane[0], plane[1]], axis=1),
                jnp.concatenate([-plane[1], plane[0]], axis=1),
            ],
            axis=0,
        )
        near = widened(jnp.concatenate([interp_one, phase_one], axis=0), 2, 2, "angle")
        meta, target, octant = leaf_plan(leaf_parent, leaf_octant, slots_one, live_leaves, tile)
        consts = (weights, band(near[:4], 0), phase_table(near[4:]), target, octant)
        return meta, consts, (band(interp_two, 1), phase_table(phase_two))

    def all_shares():
        gathered = lax.all_gather(flat(), "angle", axis=0)
        meta, consts, upper = prepared()
        return (*level_one_whole(gathered, consts, meta, slots_one), *upper)

    def two_shares():
        mine = lax.rem(me, 2)
        cells = flat()
        lefts = []

        def fetch(step, after):
            own = cells[:, step * tile : (step + 1) * tile]
            if after is not None:
                own = lax.optimization_barrier((own, after))[0]
            got = lax.ppermute(own, "angle", [(0, 2), (1, 3)])
            if lefts:
                got = lax.optimization_barrier((got, lefts[-1]))[0]
            lefts.append(jnp.where(me < 2, own, got))

        ahead = min(3, steps)
        for step in range(ahead):
            fetch(step, None)
        meta, consts, upper = prepared()
        sums = None
        for step in range(steps):
            left = lefts[step]
            right = lax.ppermute(left, "angle", [(0, 1), (1, 0), (2, 3), (3, 2)])
            places = jnp.stack([mine * steps + step, (1 - mine) * steps + step])
            marks = jnp.concatenate([meta, places.astype(jnp.int32)])
            out = level_one_pair(left, right, sums, consts, marks, tiles, slots_one)
            sums = out[0]
            if step == 0:
                carry = out[1]
            if step + ahead < steps:
                fetch(step + ahead, sums)
        return (sums, carry, *upper)

    if count == 4:
        most = lax.pmax(live_leaves, "box")
        sums, carry, bands_two, table_two = lax.cond(most <= 2 * per, two_shares, all_shares)
    else:
        sums, carry, bands_two, table_two = all_shares()
    incoming = passed_along(carry[:, 7], "box", -1)
    live = jnp.sum((box_parent != slots_two).astype(jnp.int32))
    signature_one, sums_two = level_two(
        sums,
        incoming,
        live,
        bands_two,
        table_two,
        box_parent,
        box_octant,
        slots_two,
    )
    incoming_two = passed_along(sums_two[:, -1], "box", -1)
    last_two = jnp.max(jnp.where(box_parent < slots_two, box_parent, -1))
    hit = jnp.arange(slots_two, dtype=jnp.int32)[:, None, None] == last_two
    signature_two = jnp.swapaxes(sums_two[:, :slots_two], 0, 1) + jnp.where(
        hit, incoming_two[None], 0.0
    )
    return (signature_one, signature_two)


def solution(mesh):
    in_specs = (
        P(None, None, ("box", "angle")),
        P(None, None, "angle"),
        P("box"),
        P("box"),
        P("box"),
        P("box"),
        P(None, "angle"),
        P(None, "angle"),
        P(None, "angle"),
        P(None, "angle"),
    )
    out_specs = (P("box", None, "angle"), P("box", None, "angle"))
    return jax.shard_map(body, mesh=mesh, in_specs=in_specs, out_specs=out_specs, check_vma=False)
```
